32 devices in a mesh: row: 4 (over x, core), col: 4 (over z), space: 2 (over y).
Axes of the slice: x: 2, y: 2, z: 4, core: 2. Of those that a mesh axis runs over, the one named last changes fastest.
Arguments:
- snapshots: bfloat16 [8192, 8192], P(('row', 'col'), 'space'), may hold values from -10 to 10
- ocean_mask: int32 [8192], P('space'), may hold values 0 or 1
- spread: float32 [], replicated, may hold values from 1 to 2
Outputs:
- affinity: float32 [3, 8192, 512], P(None, ('row', 'col'), 'space')
The draws below stay inside these ranges and needn't reach their ends.
All inputs are finite; a program needn't handle non-finite values. No bound on the sum of `ocean_mask` on one device may be relied on, other than what follows from the above.
Results may differ from the reference program's by a relative error of at most 0.0003.
Values may be sent and summed in bfloat16 or wider, within the bound.
A program may use at most 64 MiB of HBM per device.

```python
import math
import jax
import jax.numpy as jnp
from jax import lax

BLOCK = 512
LAG = 240
BANDS = 3
NT = 8192
NCELL = 8192
N_COL = 4


def draw_snapshots(key, part):
    times = jnp.arange(NT, dtype=jnp.float32)[:, None]
    total = jnp.zeros((NT, NCELL), jnp.float32)
    two_pi = 2.0 * math.pi
    for index in range(3):
        period = jnp.exp(jax.random.uniform(jax.random.fold_in(key, 10 + index), (1, NCELL), jnp.float32, math.log(12.0), math.log(4096.0)))
        phase = jax.random.uniform(jax.random.fold_in(key, 20 + index), (1, NCELL), jnp.float32, 0.0, two_pi)
        amplitude = jax.random.uniform(jax.random.fold_in(key, 30 + index), (1, NCELL), jnp.float32, 0.25, 0.8)
        total = total + amplitude * jnp.sin(two_pi * jnp.mod(times, period) / period + phase)
    for index in range(4):
        period = jnp.exp(jax.random.uniform(jax.random.fold_in(key, 40 + index), (1, 1), jnp.float32, math.log(168.0), math.log(8192.0)))
        phase = jax.random.uniform(jax.random.fold_in(key, 50 + index), (1, 1), jnp.float32, 0.0, two_pi)
        shape_draw = jnp.clip(jax.random.normal(jax.random.fold_in(key, 60 + index), (1, NCELL), jnp.float32), -2.5, 2.5)
        pattern = 0.5 * shape_draw
        total = total + pattern * jnp.sin(two_pi * jnp.mod(times, period) / period + phase)
    noise = 0.45 * jnp.clip(jax.random.normal(jax.random.fold_in(key, 3), (NT, NCELL), jnp.float32), -4.0, 4.0)
    return (total + noise).astype(jnp.bfloat16)


def touch_ends(entries, stream_key, smallest, high):
    shape = entries.shape
    spot = [jax.random.randint(jax.random.fold_in(stream_key, axis), (), 0, shape[axis]) for axis in range(len(shape))]
    entries = entries.at[tuple(spot)].set(smallest)
    longest = shape.index(max(shape))
    spot[longest] = (spot[longest] + 1) % shape[longest]
    return entries.at[tuple(spot)].set(high)


def setup_inputs(seed: int = 0) -> dict:
    seeds = jax.random.split(jax.random.key(seed), 4)
    snapshots = draw_snapshots(jax.random.fold_in(seeds[3], 71), 0)
    ocean_mask = touch_ends((jax.random.randint(seeds[1], (NCELL,), 0, 4) < 3).astype(jnp.int32), jax.random.fold_in(seeds[1], 1), 0, 1)
    spread = jnp.clip(jnp.exp(jax.random.uniform(seeds[2], (), jnp.float32, math.log(1.0), math.log(2.0))), 1.0, 2.0)
    return dict(snapshots=snapshots, ocean_mask=ocean_mask, spread=spread)


def combine_lags(earlier, later, extent):
    keep = earlier.shape[0] + later.shape[0] - extent - 1
    return earlier[-keep:, -keep:] + later[:keep, :keep]

def lag_sum(distance, window):
    extent = distance.shape[0]
    summed = None
    doubled = distance
    remaining = window
    while remaining:
        if remaining % 2 == 1:
            summed = doubled if summed is None else combine_lags(summed, doubled, extent)
        remaining = remaining // 2
        if remaining:
            doubled = combine_lags(doubled, doubled, extent)
    return summed

def reference(snapshots, ocean_mask, spread):
    masked = snapshots * ocean_mask.astype(jnp.bfloat16)[None, :]
    padded = jnp.concatenate([jnp.zeros((LAG - 1, NCELL), jnp.bfloat16), masked], axis=0).astype(jnp.float32)
    row_norms = lax.optimization_barrier(jnp.sum(padded * padded, axis=1))
    extent = BLOCK + LAG - 1
    nblocks = NT // BLOCK
    denominator = LAG * NCELL * spread

    def one_block(block_id):
        group_id = block_id // N_COL
        slot_id = block_id % N_COL
        row_ext = lax.dynamic_slice_in_dim(padded, (block_id * BLOCK).astype(jnp.int32), extent, 0)
        row_sq = lax.dynamic_slice_in_dim(row_norms, (block_id * BLOCK).astype(jnp.int32), extent, 0)
        band_list = []
        for band_id in range(BANDS):
            partner = group_id * N_COL + (slot_id - band_id + N_COL) % N_COL
            col_ext = lax.dynamic_slice_in_dim(padded, (partner * BLOCK).astype(jnp.int32), extent, 0)
            col_sq = lax.dynamic_slice_in_dim(row_norms, (partner * BLOCK).astype(jnp.int32), extent, 0)
            gram_tile = jnp.dot(row_ext, col_ext.T, precision=lax.Precision.HIGHEST, preferred_element_type=jnp.float32)
            distance = row_sq[:, None] + col_sq[None, :] - 2.0 * gram_tile
            band_list.append(jnp.exp(-lag_sum(distance, LAG) / denominator))
        return jnp.stack(band_list)
    block_ids = jnp.arange(nblocks, dtype=jnp.int32)
    kernel = lax.map(one_block, block_ids)
    degree = lax.optimization_barrier(jnp.sum(kernel, axis=(1, 3)))
    group_ids = block_ids // N_COL
    slot_ids = block_ids % N_COL
    col_list = []
    for band_id in range(BANDS):
        partner = group_ids * N_COL + (slot_ids - band_id + N_COL) % N_COL
        col_list.append(degree[partner])
    column_degrees = jnp.stack(col_list, axis=1)
    factor = float(BANDS * BLOCK)
    affinity = factor * kernel / jnp.sqrt(degree[:, None, :, None] * column_degrees[:, :, None, :])
    return jnp.transpose(affinity, (1, 0, 2, 3)).reshape(BANDS, NT, BLOCK)
```

```python
import jax
import jax.numpy as jnp
from jax import lax
from jax.sharding import PartitionSpec as P

LAG = 240
BANDS = 3


def passed_along(block, axis, distance):
    devices = range(lax.axis_size(axis))
    route = [(i - distance, i) for i in devices if i - distance in devices]
    return lax.ppermute(block, axis, route)


def shifted(block, axis, distance):
    devices = range(lax.axis_size(axis))
    route = [((i - distance) % len(devices), i) for i in devices]
    return lax.ppermute(block, axis, route)


def combine_lags(earlier, later, extent):
    keep = earlier.shape[0] + later.shape[0] - extent - 1
    return earlier[-keep:, -keep:] + later[:keep, :keep]


def lag_sum(distance, window):
    extent = distance.shape[0]
    summed = None
    doubled = distance
    remaining = window
    while remaining:
        if remaining % 2 == 1:
            summed = doubled if summed is None else combine_lags(summed, doubled, extent)
        remaining = remaining // 2
        if remaining:
            doubled = combine_lags(doubled, doubled, extent)
    return summed


def square_norms(values):
    return jnp.sum(jnp.square(values.astype(jnp.float32)), axis=1)


def per_device(snapshots, ocean_mask, spread):
    block_rows = snapshots.shape[0]
    cells_dev = snapshots.shape[1]
    masked = snapshots * ocean_mask.astype(jnp.bfloat16)[None, :]
    history = passed_along(masked[block_rows - (LAG - 1) :], ("row", "col"), 1)
    own_rows = jnp.concatenate([history, masked], axis=0)
    partners = [own_rows]
    current = own_rows
    for offset in range(1, BANDS):
        current = shifted(current, "col", 1)
        partners.append(current)
    row_sq = square_norms(own_rows)
    lagged_list = []
    for partner in partners:
        col_sq = square_norms(partner)
        gram_tile = lax.dot_general(
            own_rows, partner, (((1,), (1,)), ((), ())), preferred_element_type=jnp.float32
        )
        distance = row_sq[:, None] + col_sq[None, :] - 2.0 * gram_tile
        lagged_list.append(lag_sum(distance, LAG))
    partial_dist = jnp.stack(lagged_list)
    column_width = block_rows // lax.axis_size("space")
    start_col = lax.axis_index("space") * column_width
    summed_dist = lax.psum(partial_dist, "space")
    lagged = lax.dynamic_slice_in_dim(summed_dist, start_col, column_width, 2)
    total_cells = cells_dev * lax.axis_size("space")
    kernel = jnp.exp(-lagged / (LAG * total_cells * spread))
    degree = lax.psum(jnp.sum(kernel, axis=(0, 2)), "space")
    degree_list = [degree]
    current_degree = degree
    for offset in range(1, BANDS):
        current_degree = shifted(current_degree, "col", 1)
        degree_list.append(current_degree)
    column_degrees = lax.dynamic_slice_in_dim(jnp.stack(degree_list), start_col, column_width, 1)
    factor = float(BANDS * block_rows)
    return factor * kernel / jnp.sqrt(degree[None, :, None] * column_degrees[:, None, :])

CHUNKS = 2


def routed(block, axis, pairs):
    return lax.ppermute(block, axis, pairs)


def pick(condition, yes, no):
    return lax.select(jnp.broadcast_to(condition, yes.shape), yes, no)


def partial_lagged(rows, row_sq, columns, col_sq):
    gram = lax.dot_general(rows, columns, (((1,), (1,)), ((), ())), preferred_element_type=jnp.float32)
    distance = row_sq[:, None] + col_sq[None, :] - 2.0 * gram
    return lag_sum(distance, LAG)[1:, 1:]


def group_of_four(snapshots, ocean_mask, spread):
    block_rows, cells_dev = snapshots.shape
    spaces = lax.axis_size("space")
    width = block_rows // spaces
    slot = lax.axis_index("col")
    here = lax.axis_index("space")
    groups = lax.axis_size("row")
    masked = snapshots * ocean_mask.astype(jnp.bfloat16)[None, :]
    tail = masked[block_rows - LAG :]
    step = block_rows // CHUNKS
    chunks = [masked[i * step : (i + 1) * step] for i in range(CHUNKS)]

    start_2 = routed(tail, ("row", "col"), [(4 * (g - 1) + 3, 4 * g + 2) for g in range(1, groups)])
    tail2_1 = routed(tail, "col", [(2, 1)])
    before, third, third_on, first_on = [], [], [], []
    for chunk in chunks:
        got = routed(chunk, "col", [(0, 1), (1, 2), (2, 3)])
        far = routed(chunk, "col", [(3, 1)])
        before.append(got)
        third.append(far)
        third_on.append(routed(far, "col", [(1, 0)]))
        first_on.append(routed(got, "col", [(1, 2)]))
    start_1 = routed(start_2, "col", [(2, 1)])
    start_0 = routed(start_1, "col", [(1, 0)])
    start = start_0 + start_1 + start_2
    tail2_0 = routed(tail2_1, "col", [(1, 0)])
    before = jnp.concatenate(before)
    tail1_3 = routed(before[block_rows - LAG :], "col", [(2, 3)])
    third = jnp.concatenate(third)
    third_on = jnp.concatenate(third_on)
    first_on = jnp.concatenate(first_on)

    rows = jnp.concatenate([pick(slot == 0, start, before[block_rows - LAG :]), masked])
    next_tail = pick(
        slot == 1, start, pick(slot == 2, first_on[block_rows - LAG :], tail2_0 + tail1_3)
    )
    next_rows = jnp.concatenate([next_tail, before + third_on])
    last_rows = jnp.concatenate([pick(slot == 1, tail2_1, start), pick(slot == 1, third, first_on)])

    over = [(i, 1 - i) for i in range(2)]

    def halves(tile, dim):
        mine = lax.dynamic_slice_in_dim(tile, here * width, width, dim)
        other = lax.dynamic_slice_in_dim(tile, (1 - here) * width, width, dim)
        return mine + routed(other, "space", over)

    row_sq = square_norms(rows)
    lagged_0 = halves(partial_lagged(rows, row_sq, rows, row_sq), 1)
    lagged_1 = halves(partial_lagged(rows, row_sq, next_rows, square_norms(next_rows)), 1)
    tile_2 = partial_lagged(rows, row_sq, last_rows, square_norms(last_rows))
    turned = routed(halves(tile_2, 0), "col", [(1, 3), (2, 0)]).T
    inner = (slot == 1) | (slot == 2)
    lagged_2 = pick(inner, halves(tile_2, 1), turned)
    lagged = jnp.stack([lagged_0, lagged_1, lagged_2])

    kernel = jnp.exp(-lagged / (LAG * cells_dev * spaces * spread))
    half_degree = jnp.sum(kernel, axis=(0, 2))
    degree = half_degree + routed(half_degree, "space", over)
    degrees = [degree] + [shifted(degree, "col", offset) for offset in range(1, BANDS)]
    column_degrees = lax.dynamic_slice_in_dim(jnp.stack(degrees), here * width, width, 1)
    factor = float(BANDS * block_rows)
    return factor * kernel / jnp.sqrt(degree[None, :, None] * column_degrees[:, None, :])


def solution(mesh):
    placed = (P(("row", "col"), "space"), P("space"), P())
    four = mesh.shape["col"] == 4 and mesh.shape["space"] == 2
    return jax.shard_map(
        group_of_four if four else per_device,
        mesh=mesh,
        in_specs=placed,
        out_specs=P(None, ("row", "col"), "space"),
        check_vma=False,
    )
```

```python
import jax
import jax.numpy as jnp
from jax import lax
from jax.experimental import pallas as pl
from jax.experimental.pallas import tpu as pltpu
from jax.sharding import PartitionSpec as P

LAG = 240
BANDS = 3


def passed_along(block, axis, distance):
    devices = range(lax.axis_size(axis))
    route = [(i - distance, i) for i in devices if i - distance in devices]
    return lax.ppermute(block, axis, route)


def shifted(block, axis, distance):
    devices = range(lax.axis_size(axis))
    route = [((i - distance) % len(devices), i) for i in devices]
    return lax.ppermute(block, axis, route)


def combine_lags(earlier, later, extent):
    keep = earlier.shape[0] + later.shape[0] - extent - 1
    return earlier[-keep:, -keep:] + later[:keep, :keep]


def lag_sum(distance, window):
    extent = distance.shape[0]
    summed = None
    doubled = distance
    remaining = window
    while remaining:
        if remaining % 2 == 1:
            summed = doubled if summed is None else combine_lags(summed, doubled, extent)
        remaining = remaining // 2
        if remaining:
            doubled = combine_lags(doubled, doubled, extent)
    return summed


def square_norms(values):
    return jnp.sum(jnp.square(values.astype(jnp.float32)), axis=1)


def per_device(snapshots, ocean_mask, spread):
    block_rows = snapshots.shape[0]
    cells_dev = snapshots.shape[1]
    masked = snapshots * ocean_mask.astype(jnp.bfloat16)[None, :]
    history = passed_along(masked[block_rows - (LAG - 1) :], ("row", "col"), 1)
    own_rows = jnp.concatenate([history, masked], axis=0)
    partners = [own_rows]
    current = own_rows
    for offset in range(1, BANDS):
        current = shifted(current, "col", 1)
        partners.append(current)
    row_sq = square_norms(own_rows)
    lagged_list = []
    for partner in partners:
        col_sq = square_norms(partner)
        gram_tile = lax.dot_general(
            own_rows, partner, (((1,), (1,)), ((), ())), preferred_element_type=jnp.float32
        )
        distance = row_sq[:, None] + col_sq[None, :] - 2.0 * gram_tile
        lagged_list.append(lag_sum(distance, LAG))
    partial_dist = jnp.stack(lagged_list)
    column_width = block_rows // lax.axis_size("space")
    start_col = lax.axis_index("space") * column_width
    summed_dist = lax.psum(partial_dist, "space")
    lagged = lax.dynamic_slice_in_dim(summed_dist, start_col, column_width, 2)
    total_cells = cells_dev * lax.axis_size("space")
    kernel = jnp.exp(-lagged / (LAG * total_cells * spread))
    degree = lax.psum(jnp.sum(kernel, axis=(0, 2)), "space")
    degree_list = [degree]
    current_degree = degree
    for offset in range(1, BANDS):
        current_degree = shifted(current_degree, "col", 1)
        degree_list.append(current_degree)
    column_degrees = lax.dynamic_slice_in_dim(jnp.stack(degree_list), start_col, column_width, 1)
    factor = float(BANDS * block_rows)
    return factor * kernel / jnp.sqrt(degree[None, :, None] * column_degrees[:, None, :])

CHUNK = 64
PIECE = 80


def gather_kernel(own, before, extra, start, tail, sent, got_before, got_extra, got_start, got_tail):
    row, slot, here = lax.axis_index("row"), lax.axis_index("col"), lax.axis_index("space")
    groups = lax.axis_size("row")
    rows = own.shape[0]
    first = rows - LAG
    n_chunk, n_piece = rows // CHUNK, LAG // PIECE
    barrier = pltpu.get_barrier_semaphore()

    def greet(group, place):
        pl.semaphore_signal(
            barrier, inc=1, device_id=(group, place, here), device_id_type=pl.DeviceIdType.MESH
        )

    def chunk(ref, c):
        return ref.at[pl.ds(c * CHUNK, CHUNK)]

    def piece(ref, p, offset=0):
        return ref.at[pl.ds(offset + p * PIECE, PIECE)]

    def copy(src, dst, kind, i, got, group, place):
        return pltpu.make_async_remote_copy(
            src_ref=src,
            dst_ref=dst,
            send_sem=sent.at[kind, i],
            recv_sem=got.at[i],
            device_id=(group, place, here),
            device_id_type=pl.DeviceIdType.MESH,
        )

    def send_chunk(src, dst, c, kind, got, place):
        made = copy(chunk(src, c), chunk(dst, c), kind, c, got, row, place)
        made.start()
        return made

    def send_piece(src, dst, p, kind, got, group, place, offset=0):
        made = copy(piece(src, p, offset), piece(dst, p), kind, p, got, group, place)
        made.start()
        return made

    def wait_chunk(dst, c, got):
        copy(chunk(dst, c), chunk(dst, c), 0, c, got, row, slot).wait_recv()

    def wait_piece(dst, p, got):
        copy(piece(dst, p), piece(dst, p), 0, p, got, row, slot).wait_recv()

    def all_sent(made):
        for one in made:
            one.wait_send()

    @pl.when(slot == 0)
    def _():
        greet(row, 1)
        pl.semaphore_wait(barrier, 1)
        made = [send_chunk(own, before, c, 0, got_before, 1) for c in range(n_chunk)]
        for c in range(n_chunk):
            wait_chunk(extra, c, got_extra)
        for p in range(n_piece):
            wait_piece(tail, p, got_tail)

        @pl.when(row > 0)
        def _():
            for p in range(n_piece):
                wait_piece(start, p, got_start)

        all_sent(made)

    @pl.when(slot == 1)
    def _():
        greet(row, 0)
        greet(row, 2)
        greet(row, 3)
        pl.semaphore_wait(barrier, 3)
        made = [send_chunk(own, before, c, 0, got_before, 2) for c in range(n_chunk)]
        for c in range(n_chunk):
            wait_chunk(extra, c, got_extra)
            made.append(send_chunk(extra, extra, c, 1, got_extra, 0))
            wait_chunk(before, c, got_before)
            made.append(send_chunk(before, extra, c, 2, got_extra, 2))
        for p in range(n_piece):
            wait_piece(tail, p, got_tail)
            made.append(send_piece(tail, tail, p, 3, got_tail, row, 0))

        @pl.when(row > 0)
        def _():
            more = []
            for p in range(n_piece):
                wait_piece(start, p, got_start)
                more.append(send_piece(start, start, p, 4, got_start, row, 0))
            all_sent(more)

        all_sent(made)

    @pl.when(slot == 2)
    def _():
        greet(row, 1)
        greet(row, 3)

        @pl.when(row > 0)
        def _():
            greet(row - 1, 3)

        pl.semaphore_wait(barrier, 2 + (row > 0).astype(jnp.int32))
        made = [send_chunk(own, before, c, 0, got_before, 3) for c in range(n_chunk)]

        @pl.when(row > 0)
        def _():
            more = []
            for p in range(n_piece):
                wait_piece(start, p, got_start)
                more.append(send_piece(start, start, p, 4, got_start, row, 1))
            all_sent(more)

        made += [send_piece(own, tail, p, 3, got_tail, row, 1, first) for p in range(n_piece)]
        for c in range(n_chunk):
            wait_chunk(before, c, got_before)
        made += [send_piece(before, tail, p, 1, got_tail, row, 3, first) for p in range(n_piece)]
        for c in range(n_chunk):
            wait_chunk(extra, c, got_extra)
        all_sent(made)

    @pl.when(slot == 3)
    def _():
        greet(row, 1)
        greet(row, 2)

        @pl.when(row < groups - 1)
        def _():
            greet(row + 1, 2)

        pl.semaphore_wait(barrier, 2 + (row < groups - 1).astype(jnp.int32))
        made = [send_chunk(own, extra, c, 0, got_extra, 1) for c in range(n_chunk)]

        @pl.when(row < groups - 1)
        def _():
            all_sent(
                [send_piece(own, start, p, 4, got_start, row + 1, 2, first) for p in range(n_piece)]
            )

        for c in range(n_chunk):
            wait_chunk(before, c, got_before)
        for p in range(n_piece):
            wait_piece(tail, p, got_tail)
        all_sent(made)


def gather_blocks(masked):
    rows, cells = masked.shape
    n_chunk, n_piece = rows // CHUNK, LAG // PIECE
    block = jax.ShapeDtypeStruct((rows, cells), masked.dtype)
    part = jax.ShapeDtypeStruct((LAG, cells), masked.dtype)
    anywhere = pl.BlockSpec(memory_space=pl.ANY)
    return pl.pallas_call(
        gather_kernel,
        out_shape=[block, block, part, part],
        in_specs=[anywhere],
        out_specs=[anywhere] * 4,
        scratch_shapes=[
            pltpu.SemaphoreType.DMA((5, n_chunk)),
            pltpu.SemaphoreType.DMA((n_chunk,)),
            pltpu.SemaphoreType.DMA((n_chunk,)),
            pltpu.SemaphoreType.DMA((n_piece,)),
            pltpu.SemaphoreType.DMA((n_piece,)),
        ],
        compiler_params=pltpu.CompilerParams(collective_id=0, has_side_effects=True),
    )(masked)


def routed(block, axis, pairs):
    return lax.ppermute(block, axis, pairs)


def pick(condition, yes, no):
    return lax.select(jnp.broadcast_to(condition, yes.shape), yes, no)


def partial_lagged(rows, row_sq, columns, col_sq):
    gram = lax.dot_general(rows, columns, (((1,), (1,)), ((), ())), preferred_element_type=jnp.float32)
    distance = row_sq[:, None] + col_sq[None, :] - 2.0 * gram
    return lag_sum(distance, LAG)[1:, 1:]


def group_of_four(snapshots, ocean_mask, spread):
    block_rows, cells_dev = snapshots.shape
    spaces = lax.axis_size("space")
    width = block_rows // spaces
    slot = lax.axis_index("col")
    here = lax.axis_index("space")
    masked = snapshots * ocean_mask.astype(jnp.bfloat16)[None, :]
    before, extra, start, tail = gather_blocks(masked)
    start = pick(lax.axis_index("row") == 0, jnp.zeros_like(start), start)
    before_tail, extra_tail = before[block_rows - LAG :], extra[block_rows - LAG :]
    rows = jnp.concatenate([pick(slot == 0, start, before_tail), masked])
    next_tail = pick(slot == 1, start, pick(slot == 2, extra_tail, tail))
    next_rows = jnp.concatenate([next_tail, pick(slot == 0, extra, before)])
    last_rows = jnp.concatenate([pick(slot == 1, tail, start), extra])

    over = [(i, 1 - i) for i in range(2)]

    def halves(tile, dim):
        mine = lax.dynamic_slice_in_dim(tile, here * width, width, dim)
        other = lax.dynamic_slice_in_dim(tile, (1 - here) * width, width, dim)
        return mine + routed(other, "space", over)

    row_sq = square_norms(rows)
    lagged_0 = halves(partial_lagged(rows, row_sq, rows, row_sq), 1)
    lagged_1 = halves(partial_lagged(rows, row_sq, next_rows, square_norms(next_rows)), 1)
    tile_2 = partial_lagged(rows, row_sq, last_rows, square_norms(last_rows))
    turned = routed(halves(tile_2, 0), "col", [(1, 3), (2, 0)]).T
    inner = (slot == 1) | (slot == 2)
    lagged_2 = pick(inner, halves(tile_2, 1), turned)
    lagged = jnp.stack([lagged_0, lagged_1, lagged_2])

    kernel = jnp.exp(-lagged / (LAG * cells_dev * spaces * spread))
    half_degree = jnp.sum(kernel, axis=(0, 2))
    degree = half_degree + routed(half_degree, "space", over)
    degrees = [degree] + [shifted(degree, "col", offset) for offset in range(1, BANDS)]
    column_degrees = lax.dynamic_slice_in_dim(jnp.stack(degrees), here * width, width, 1)
    factor = float(BANDS * block_rows)
    return factor * kernel / jnp.sqrt(degree[None, :, None] * column_degrees[:, None, :])


def solution(mesh):
    placed = (P(("row", "col"), "space"), P("space"), P())
    four = mesh.shape["col"] == 4 and mesh.shape["space"] == 2
    return jax.shard_map(
        group_of_four if four else per_device,
        mesh=mesh,
        in_specs=placed,
        out_specs=P(None, ("row", "col"), "space"),
        check_vma=False,
    )
```

```python
import jax
import jax.numpy as jnp
from jax import lax
from jax.experimental import pallas as pl
from jax.experimental.pallas import tpu as pltpu
from jax.sharding import PartitionSpec as P

LAG = 240
BANDS = 3


def passed_along(block, axis, distance):
    devices = range(lax.axis_size(axis))
    route = [(i - distance, i) for i in devices if i - distance in devices]
    return lax.ppermute(block, axis, route)


def shifted(block, axis, distance):
    devices = range(lax.axis_size(axis))
    route = [((i - distance) % len(devices), i) for i in devices]
    return lax.ppermute(block, axis, route)


def combine_lags(earlier, later, extent):
    keep = earlier.shape[0] + later.shape[0] - extent - 1
    return earlier[-keep:, -keep:] + later[:keep, :keep]


def lag_sum(distance, window):
    extent = distance.shape[0]
    summed = None
    doubled = distance
    remaining = window
    while remaining:
        if remaining % 2 == 1:
            summed = doubled if summed is None else combine_lags(summed, doubled, extent)
        remaining = remaining // 2
        if remaining:
            doubled = combine_lags(doubled, doubled, extent)
    return summed


def square_norms(values):
    return jnp.sum(jnp.square(values.astype(jnp.float32)), axis=1)


def per_device(snapshots, ocean_mask, spread):
    block_rows = snapshots.shape[0]
    cells_dev = snapshots.shape[1]
    masked = snapshots * ocean_mask.astype(jnp.bfloat16)[None, :]
    history = passed_along(masked[block_rows - (LAG - 1) :], ("row", "col"), 1)
    own_rows = jnp.concatenate([history, masked], axis=0)
    partners = [own_rows]
    current = own_rows
    for offset in range(1, BANDS):
        current = shifted(current, "col", 1)
        partners.append(current)
    row_sq = square_norms(own_rows)
    lagged_list = []
    for partner in partners:
        col_sq = square_norms(partner)
        gram_tile = lax.dot_general(
            own_rows, partner, (((1,), (1,)), ((), ())), preferred_element_type=jnp.float32
        )
        distance = row_sq[:, None] + col_sq[None, :] - 2.0 * gram_tile
        lagged_list.append(lag_sum(distance, LAG))
    partial_dist = jnp.stack(lagged_list)
    column_width = block_rows // lax.axis_size("space")
    start_col = lax.axis_index("space") * column_width
    summed_dist = lax.psum(partial_dist, "space")
    lagged = lax.dynamic_slice_in_dim(summed_dist, start_col, column_width, 2)
    total_cells = cells_dev * lax.axis_size("space")
    kernel = jnp.exp(-lagged / (LAG * total_cells * spread))
    degree = lax.psum(jnp.sum(kernel, axis=(0, 2)), "space")
    degree_list = [degree]
    current_degree = degree
    for offset in range(1, BANDS):
        current_degree = shifted(current_degree, "col", 1)
        degree_list.append(current_degree)
    column_degrees = lax.dynamic_slice_in_dim(jnp.stack(degree_list), start_col, column_width, 1)
    factor = float(BANDS * block_rows)
    return factor * kernel / jnp.sqrt(degree[None, :, None] * column_degrees[:, None, :])

CHUNK = 64
PIECE = 80


def gather_kernel(own, before, extra, start, tail, sent, got_before, got_extra, got_start, got_tail):
    row, slot, here = lax.axis_index("row"), lax.axis_index("col"), lax.axis_index("space")
    groups = lax.axis_size("row")
    rows = own.shape[0]
    first = rows - LAG
    n_chunk, n_piece = rows // CHUNK, LAG // PIECE
    barrier = pltpu.get_barrier_semaphore()

    def greet(group, place):
        pl.semaphore_signal(
            barrier, inc=1, device_id=(group, place, here), device_id_type=pl.DeviceIdType.MESH
        )

    def chunk(ref, c):
        return ref.at[pl.ds(c * CHUNK, CHUNK)]

    def piece(ref, p, offset=0):
        return ref.at[pl.ds(offset + p * PIECE, PIECE)]

    def copy(src, dst, kind, i, got, group, place):
        return pltpu.make_async_remote_copy(
            src_ref=src,
            dst_ref=dst,
            send_sem=sent.at[kind, i],
            recv_sem=got.at[i],
            device_id=(group, place, here),
            device_id_type=pl.DeviceIdType.MESH,
        )

    def send_chunk(src, dst, c, kind, got, place):
        made = copy(chunk(src, c), chunk(dst, c), kind, c, got, row, place)
        made.start()
        return made

    def send_piece(src, dst, p, kind, got, group, place, offset=0):
        made = copy(piece(src, p, offset), piece(dst, p), kind, p, got, group, place)
        made.start()
        return made

    def wait_chunk(dst, c, got):
        copy(chunk(dst, c), chunk(dst, c), 0, c, got, row, slot).wait_recv()

    def wait_piece(dst, p, got):
        copy(piece(dst, p), piece(dst, p), 0, p, got, row, slot).wait_recv()

    def all_sent(made):
        for one in made:
            one.wait_send()

    @pl.when(slot == 0)
    def _():
        greet(row, 1)
        pl.semaphore_wait(barrier, 1)
        made = [send_chunk(own, before, c, 0, got_before, 1) for c in range(n_chunk)]
        for c in range(n_chunk):
            wait_chunk(extra, c, got_extra)
        for p in range(n_piece):
            wait_piece(tail, p, got_tail)

        @pl.when(row > 0)
        def _():
            for p in range(n_piece):
                wait_piece(start, p, got_start)

        all_sent(made)

    @pl.when(slot == 1)
    def _():
        greet(row, 0)
        greet(row, 2)
        greet(row, 3)
        pl.semaphore_wait(barrier, 3)
        made = [send_chunk(own, before, c, 0, got_before, 2) for c in range(n_chunk)]
        for c in range(n_chunk):
            wait_chunk(extra, c, got_extra)
            made.append(send_chunk(extra, extra, c, 1, got_extra, 0))
            wait_chunk(before, c, got_before)
            made.append(send_chunk(before, extra, c, 2, got_extra, 2))
            p = (c - 1) // 2
            if c % 2 == 1 and p < n_piece:
                wait_piece(tail, p, got_tail)
                made.append(send_piece(tail, tail, p, 3, got_tail, row, 0))
            p = (c - 2) // 2
            if c % 2 == 0 and 0 <= p < n_piece:

                @pl.when(row > 0)
                def _():
                    wait_piece(start, p, got_start)
                    send_piece(start, start, p, 4, got_start, row, 0)

        @pl.when(row > 0)
        def _():
            for p in range(n_piece):
                copy(piece(start, p), piece(start, p), 4, p, got_start, row, 0).wait_send()

        all_sent(made)

    @pl.when(slot == 2)
    def _():
        greet(row, 1)
        greet(row, 3)

        @pl.when(row > 0)
        def _():
            greet(row - 1, 3)

        pl.semaphore_wait(barrier, 2 + (row > 0).astype(jnp.int32))
        made = [send_chunk(own, before, c, 0, got_before, 3) for c in range(n_chunk)]
        made += [send_piece(own, tail, p, 3, got_tail, row, 1, first) for p in range(n_piece)]

        @pl.when(row > 0)
        def _():
            for p in range(n_piece):
                wait_piece(start, p, got_start)
                send_piece(start, start, p, 4, got_start, row, 1)

        for c in range(n_chunk):
            wait_chunk(before, c, got_before)
        made += [send_piece(before, tail, p, 1, got_tail, row, 3, first) for p in range(n_piece)]
        for c in range(n_chunk):
            wait_chunk(extra, c, got_extra)

        @pl.when(row > 0)
        def _():
            for p in range(n_piece):
                copy(piece(start, p), piece(start, p), 4, p, got_start, row, 1).wait_send()

        all_sent(made)

    @pl.when(slot == 3)
    def _():
        greet(row, 1)
        greet(row, 2)

        @pl.when(row < groups - 1)
        def _():
            greet(row + 1, 2)

        pl.semaphore_wait(barrier, 2 + (row < groups - 1).astype(jnp.int32))

        @pl.when(row < groups - 1)
        def _():
            for p in range(n_piece):
                send_piece(own, start, p, 4, got_start, row + 1, 2, first)

        made = [send_chunk(own, extra, c, 0, got_extra, 1) for c in range(n_chunk)]
        for c in range(n_chunk):
            wait_chunk(before, c, got_before)
        for p in range(n_piece):
            wait_piece(tail, p, got_tail)

        @pl.when(row < groups - 1)
        def _():
            for p in range(n_piece):
                sent_piece = piece(own, p, first)
                copy(sent_piece, piece(start, p), 4, p, got_start, row + 1, 2).wait_send()

        all_sent(made)


def gather_blocks(masked):
    rows, cells = masked.shape
    n_chunk, n_piece = rows // CHUNK, LAG // PIECE
    block = jax.ShapeDtypeStruct((rows, cells), masked.dtype)
    part = jax.ShapeDtypeStruct((LAG, cells), masked.dtype)
    anywhere = pl.BlockSpec(memory_space=pl.ANY)
    return pl.pallas_call(
        gather_kernel,
        out_shape=[block, block, part, part],
        in_specs=[anywhere],
        out_specs=[anywhere] * 4,
        scratch_shapes=[
            pltpu.SemaphoreType.DMA((5, n_chunk)),
            pltpu.SemaphoreType.DMA((n_chunk,)),
            pltpu.SemaphoreType.DMA((n_chunk,)),
            pltpu.SemaphoreType.DMA((n_piece,)),
            pltpu.SemaphoreType.DMA((n_piece,)),
        ],
        compiler_params=pltpu.CompilerParams(collective_id=0, has_side_effects=True),
    )(masked)


def routed(block, axis, pairs):
    return lax.ppermute(block, axis, pairs)


def pick(condition, yes, no):
    return lax.select(jnp.broadcast_to(condition, yes.shape), yes, no)


def partial_lagged(rows, row_sq, columns, col_sq):
    gram = lax.dot_general(rows, columns, (((1,), (1,)), ((), ())), preferred_element_type=jnp.float32)
    distance = row_sq[:, None] + col_sq[None, :] - 2.0 * gram
    return lag_sum(distance, LAG)[1:, 1:]


def group_of_four(snapshots, ocean_mask, spread):
    block_rows, cells_dev = snapshots.shape
    spaces = lax.axis_size("space")
    width = block_rows // spaces
    slot = lax.axis_index("col")
    here = lax.axis_index("space")
    masked = snapshots * ocean_mask.astype(jnp.bfloat16)[None, :]
    before, extra, start, tail = gather_blocks(masked)
    start = pick(lax.axis_index("row") == 0, jnp.zeros_like(start), start)
    before_tail, extra_tail = before[block_rows - LAG :], extra[block_rows - LAG :]
    rows = jnp.concatenate([pick(slot == 0, start, before_tail), masked])
    next_tail = pick(slot == 1, start, pick(slot == 2, extra_tail, tail))
    next_rows = jnp.concatenate([next_tail, pick(slot == 0, extra, before)])
    last_rows = jnp.concatenate([pick(slot == 1, tail, start), extra])

    over = [(i, 1 - i) for i in range(2)]

    def halves(tile, dim):
        mine = lax.dynamic_slice_in_dim(tile, here * width, width, dim)
        other = lax.dynamic_slice_in_dim(tile, (1 - here) * width, width, dim)
        return mine + routed(other, "space", over)

    row_sq = square_norms(rows)
    tile_2 = partial_lagged(rows, row_sq, last_rows, square_norms(last_rows))
    tile_2, rows, next_rows = lax.optimization_barrier((tile_2, rows, next_rows))
    turned = routed(halves(tile_2, 0), "col", [(1, 3), (2, 0)]).T
    lagged_0 = halves(partial_lagged(rows, row_sq, rows, row_sq), 1)
    lagged_1 = halves(partial_lagged(rows, row_sq, next_rows, square_norms(next_rows)), 1)
    inner = (slot == 1) | (slot == 2)
    lagged_2 = pick(inner, halves(tile_2, 1), turned)
    lagged = jnp.stack([lagged_0, lagged_1, lagged_2])

    kernel = jnp.exp(-lagged / (LAG * cells_dev * spaces * spread))
    half_degree = jnp.sum(kernel, axis=(0, 2))
    degree = half_degree + routed(half_degree, "space", over)
    degrees = [degree] + [shifted(degree, "col", offset) for offset in range(1, BANDS)]
    column_degrees = lax.dynamic_slice_in_dim(jnp.stack(degrees), here * width, width, 1)
    factor = float(BANDS * block_rows)
    return factor * kernel / jnp.sqrt(degree[None, :, None] * column_degrees[:, None, :])


def solution(mesh):
    placed = (P(("row", "col"), "space"), P("space"), P())
    four = mesh.shape["col"] == 4 and mesh.shape["space"] == 2
    return jax.shard_map(
        group_of_four if four else per_device,
        mesh=mesh,
        in_specs=placed,
        out_specs=P(None, ("row", "col"), "space"),
        check_vma=False,
    )
```

```python
import jax
import jax.numpy as jnp
from jax import lax
from jax.experimental import pallas as pl
from jax.experimental.pallas import tpu as pltpu
from jax.sharding import PartitionSpec as P

LAG = 240
BANDS = 3


def passed_along(block, axis, distance):
    devices = range(lax.axis_size(axis))
    route = [(i - distance, i) for i in devices if i - distance in devices]
    return lax.ppermute(block, axis, route)


def shifted(block, axis, distance):
    devices = range(lax.axis_size(axis))
    route = [((i - distance) % len(devices), i) for i in devices]
    return lax.ppermute(block, axis, route)


def combine_lags(earlier, later, extent):
    keep = earlier.shape[0] + later.shape[0] - extent - 1
    return earlier[-keep:, -keep:] + later[:keep, :keep]


def lag_sum(distance, window):
    extent = distance.shape[0]
    summed = None
    doubled = distance
    remaining = window
    while remaining:
        if remaining % 2 == 1:
            summed = doubled if summed is None else combine_lags(summed, doubled, extent)
        remaining = remaining // 2
        if remaining:
            doubled = combine_lags(doubled, doubled, extent)
    return summed


def square_norms(values):
    return jnp.sum(jnp.square(values.astype(jnp.float32)), axis=1)


def per_device(snapshots, ocean_mask, spread):
    block_rows = snapshots.shape[0]
    cells_dev = snapshots.shape[1]
    masked = snapshots * ocean_mask.astype(jnp.bfloat16)[None, :]
    history = passed_along(masked[block_rows - (LAG - 1) :], ("row", "col"), 1)
    own_rows = jnp.concatenate([history, masked], axis=0)
    partners = [own_rows]
    current = own_rows
    for offset in range(1, BANDS):
        current = shifted(current, "col", 1)
        partners.append(current)
    row_sq = square_norms(own_rows)
    lagged_list = []
    for partner in partners:
        col_sq = square_norms(partner)
        gram_tile = lax.dot_general(
            own_rows, partner, (((1,), (1,)), ((), ())), preferred_element_type=jnp.float32
        )
        distance = row_sq[:, None] + col_sq[None, :] - 2.0 * gram_tile
        lagged_list.append(lag_sum(distance, LAG))
    partial_dist = jnp.stack(lagged_list)
    column_width = block_rows // lax.axis_size("space")
    start_col = lax.axis_index("space") * column_width
    summed_dist = lax.psum(partial_dist, "space")
    lagged = lax.dynamic_slice_in_dim(summed_dist, start_col, column_width, 2)
    total_cells = cells_dev * lax.axis_size("space")
    kernel = jnp.exp(-lagged / (LAG * total_cells * spread))
    degree = lax.psum(jnp.sum(kernel, axis=(0, 2)), "space")
    degree_list = [degree]
    current_degree = degree
    for offset in range(1, BANDS):
        current_degree = shifted(current_degree, "col", 1)
        degree_list.append(current_degree)
    column_degrees = lax.dynamic_slice_in_dim(jnp.stack(degree_list), start_col, column_width, 1)
    factor = float(BANDS * block_rows)
    return factor * kernel / jnp.sqrt(degree[None, :, None] * column_degrees[:, None, :])

CHUNK = 64
PIECE = 80


def gather_kernel(own, before, extra, start, tail, sent, got_before, got_extra, got_start, got_tail):
    row, slot, here = lax.axis_index("row"), lax.axis_index("col"), lax.axis_index("space")
    groups = lax.axis_size("row")
    rows = own.shape[0]
    first = rows - LAG
    n_chunk, n_piece = rows // CHUNK, LAG // PIECE
    barrier = pltpu.get_barrier_semaphore()

    def greet(group, place):
        pl.semaphore_signal(
            barrier, inc=1, device_id=(group, place, here), device_id_type=pl.DeviceIdType.MESH
        )

    def chunk(ref, c):
        return ref.at[pl.ds(c * CHUNK, CHUNK)]

    def piece(ref, p, offset=0):
        return ref.at[pl.ds(offset + p * PIECE, PIECE)]

    def copy(src, dst, kind, i, got, group, place):
        return pltpu.make_async_remote_copy(
            src_ref=src,
            dst_ref=dst,
            send_sem=sent.at[kind, i],
            recv_sem=got.at[i],
            device_id=(group, place, here),
            device_id_type=pl.DeviceIdType.MESH,
        )

    def send_chunk(src, dst, c, kind, got, place):
        made = copy(chunk(src, c), chunk(dst, c), kind, c, got, row, place)
        made.start()
        return made

    def send_piece(src, dst, p, kind, got, group, place, offset=0):
        made = copy(piece(src, p, offset), piece(dst, p), kind, p, got, group, place)
        made.start()
        return made

    def wait_chunk(dst, c, got):
        copy(chunk(dst, c), chunk(dst, c), 0, c, got, row, slot).wait_recv()

    def wait_piece(dst, p, got):
        copy(piece(dst, p), piece(dst, p), 0, p, got, row, slot).wait_recv()

    def all_sent(made):
        for one in made:
            one.wait_send()

    @pl.when(slot == 0)
    def _():
        greet(row, 1)
        pl.semaphore_wait(barrier, 1)
        made = [send_chunk(own, before, c, 0, got_before, 1) for c in range(n_chunk)]
        for c in range(n_chunk):
            wait_chunk(extra, c, got_extra)
        for p in range(n_piece):
            wait_piece(tail, p, got_tail)

        @pl.when(row > 0)
        def _():
            for p in range(n_piece):
                wait_piece(start, p, got_start)

        all_sent(made)

    @pl.when(slot == 1)
    def _():
        greet(row, 0)
        greet(row, 2)
        greet(row, 3)
        pl.semaphore_wait(barrier, 3)
        made = [send_chunk(own, before, c, 0, got_before, 2) for c in range(n_chunk)]
        for c in range(n_chunk):
            wait_chunk(extra, c, got_extra)
            made.append(send_chunk(extra, extra, c, 1, got_extra, 0))
            wait_chunk(before, c, got_before)
            made.append(send_chunk(before, extra, c, 2, got_extra, 2))
            p = (c - 3) // 2
            if c % 2 == 1 and 0 <= p < n_piece:
                wait_piece(tail, p, got_tail)
                made.append(send_piece(tail, tail, p, 3, got_tail, row, 0))

        @pl.when(row > 0)
        def _():
            more = []
            for p in range(n_piece):
                wait_piece(start, p, got_start)
                more.append(send_piece(start, start, p, 4, got_start, row, 0))
            all_sent(more)

        all_sent(made)

    @pl.when(slot == 2)
    def _():
        greet(row, 1)
        greet(row, 3)

        @pl.when(row > 0)
        def _():
            greet(row - 1, 3)

        pl.semaphore_wait(barrier, 2 + (row > 0).astype(jnp.int32))
        made = [send_piece(own, tail, p, 3, got_tail, row, 1, first) for p in range(n_piece)]
        made += [send_chunk(own, before, c, 0, got_before, 3) for c in range(n_chunk)]

        @pl.when(row > 0)
        def _():
            for p in range(n_piece):
                wait_piece(start, p, got_start)
                send_piece(start, start, p, 4, got_start, row, 1)

        for c in range(n_chunk):
            wait_chunk(before, c, got_before)
        made += [send_piece(before, tail, p, 1, got_tail, row, 3, first) for p in range(n_piece)]
        for c in range(n_chunk):
            wait_chunk(extra, c, got_extra)

        @pl.when(row > 0)
        def _():
            for p in range(n_piece):
                copy(piece(start, p), piece(start, p), 4, p, got_start, row, 1).wait_send()

        all_sent(made)

    @pl.when(slot == 3)
    def _():
        greet(row, 1)
        greet(row, 2)

        @pl.when(row < groups - 1)
        def _():
            greet(row + 1, 2)

        pl.semaphore_wait(barrier, 2 + (row < groups - 1).astype(jnp.int32))
        made = [send_chunk(own, extra, c, 0, got_extra, 1) for c in range(n_chunk)]

        @pl.when(row < groups - 1)
        def _():
            all_sent(
                [send_piece(own, start, p, 4, got_start, row + 1, 2, first) for p in range(n_piece)]
            )

        for c in range(n_chunk):
            wait_chunk(before, c, got_before)
        for p in range(n_piece):
            wait_piece(tail, p, got_tail)
        all_sent(made)


def gather_blocks(masked):
    rows, cells = masked.shape
    n_chunk, n_piece = rows // CHUNK, LAG // PIECE
    block = jax.ShapeDtypeStruct((rows, cells), masked.dtype)
    part = jax.ShapeDtypeStruct((LAG, cells), masked.dtype)
    anywhere = pl.BlockSpec(memory_space=pl.ANY)
    return pl.pallas_call(
        gather_kernel,
        out_shape=[block, block, part, part],
        in_specs=[anywhere],
        out_specs=[anywhere] * 4,
        scratch_shapes=[
            pltpu.SemaphoreType.DMA((5, n_chunk)),
            pltpu.SemaphoreType.DMA((n_chunk,)),
            pltpu.SemaphoreType.DMA((n_chunk,)),
            pltpu.SemaphoreType.DMA((n_piece,)),
            pltpu.SemaphoreType.DMA((n_piece,)),
        ],
        compiler_params=pltpu.CompilerParams(collective_id=0, has_side_effects=True),
    )(masked)


def routed(block, axis, pairs):
    return lax.ppermute(block, axis, pairs)


def pick(condition, yes, no):
    return lax.select(jnp.broadcast_to(condition, yes.shape), yes, no)


def partial_lagged(rows, row_sq, columns, col_sq):
    gram = lax.dot_general(rows, columns, (((1,), (1,)), ((), ())), preferred_element_type=jnp.float32)
    distance = row_sq[:, None] + col_sq[None, :] - 2.0 * gram
    return lag_sum(distance, LAG)[1:, 1:]


def group_of_four(snapshots, ocean_mask, spread):
    block_rows, cells_dev = snapshots.shape
    spaces = lax.axis_size("space")
    width = block_rows // spaces
    slot = lax.axis_index("col")
    here = lax.axis_index("space")
    masked = snapshots * ocean_mask.astype(jnp.bfloat16)[None, :]
    before, extra, start, tail = gather_blocks(masked)
    start = pick(lax.axis_index("row") == 0, jnp.zeros_like(start), start)
    before_tail, extra_tail = before[block_rows - LAG :], extra[block_rows - LAG :]
    rows = jnp.concatenate([pick(slot == 0, start, before_tail), masked])
    next_tail = pick(slot == 1, start, pick(slot == 2, extra_tail, tail))
    next_rows = jnp.concatenate([next_tail, pick(slot == 0, extra, before)])
    last_rows = jnp.concatenate([pick(slot == 1, tail, start), extra])

    over = [(i, 1 - i) for i in range(2)]

    def halves(tile, dim):
        mine = lax.dynamic_slice_in_dim(tile, here * width, width, dim)
        other = lax.dynamic_slice_in_dim(tile, (1 - here) * width, width, dim)
        return mine + routed(other, "space", over)

    row_sq = square_norms(rows)
    lagged_0 = halves(partial_lagged(rows, row_sq, rows, row_sq), 1)
    lagged_1 = halves(partial_lagged(rows, row_sq, next_rows, square_norms(next_rows)), 1)
    tile_2 = partial_lagged(rows, row_sq, last_rows, square_norms(last_rows))
    turned = routed(halves(tile_2, 0), "col", [(1, 3), (2, 0)]).T
    inner = (slot == 1) | (slot == 2)
    lagged_2 = pick(inner, halves(tile_2, 1), turned)
    lagged = jnp.stack([lagged_0, lagged_1, lagged_2])

    kernel = jnp.exp(-lagged / (LAG * cells_dev * spaces * spread))
    half_degree = jnp.sum(kernel, axis=(0, 2))
    degree = half_degree + routed(half_degree, "space", over)
    degrees = [degree] + [shifted(degree, "col", offset) for offset in range(1, BANDS)]
    column_degrees = lax.dynamic_slice_in_dim(jnp.stack(degrees), here * width, width, 1)
    factor = float(BANDS * block_rows)
    return factor * kernel / jnp.sqrt(degree[None, :, None] * column_degrees[:, None, :])


def solution(mesh):
    placed = (P(("row", "col"), "space"), P("space"), P())
    four = mesh.shape["col"] == 4 and mesh.shape["space"] == 2
    return jax.shard_map(
        group_of_four if four else per_device,
        mesh=mesh,
        in_specs=placed,
        out_specs=P(None, ("row", "col"), "space"),
        check_vma=False,
    )
```

```python
import jax
import jax.numpy as jnp
from jax import lax
from jax.experimental import pallas as pl
from jax.experimental.pallas import tpu as pltpu
from jax.sharding import PartitionSpec as P

LAG = 240
BANDS = 3


def passed_along(block, axis, distance):
    devices = range(lax.axis_size(axis))
    route = [(i - distance, i) for i in devices if i - distance in devices]
    return lax.ppermute(block, axis, route)


def shifted(block, axis, distance):
    devices = range(lax.axis_size(axis))
    route = [((i - distance) % len(devices), i) for i in devices]
    return lax.ppermute(block, axis, route)


def combine_lags(earlier, later, extent):
    keep = earlier.shape[0] + later.shape[0] - extent - 1
    return earlier[-keep:, -keep:] + later[:keep, :keep]


def lag_sum(distance, window):
    extent = distance.shape[0]
    summed = None
    doubled = distance
    remaining = window
    while remaining:
        if remaining % 2 == 1:
            summed = doubled if summed is None else combine_lags(summed, doubled, extent)
        remaining = remaining // 2
        if remaining:
            doubled = combine_lags(doubled, doubled, extent)
    return summed


def square_norms(values):
    return jnp.sum(jnp.square(values.astype(jnp.float32)), axis=1)


def per_device(snapshots, ocean_mask, spread):
    block_rows = snapshots.shape[0]
    cells_dev = snapshots.shape[1]
    masked = snapshots * ocean_mask.astype(jnp.bfloat16)[None, :]
    history = passed_along(masked[block_rows - (LAG - 1) :], ("row", "col"), 1)
    own_rows = jnp.concatenate([history, masked], axis=0)
    partners = [own_rows]
    current = own_rows
    for offset in range(1, BANDS):
        current = shifted(current, "col", 1)
        partners.append(current)
    row_sq = square_norms(own_rows)
    lagged_list = []
    for partner in partners:
        col_sq = square_norms(partner)
        gram_tile = lax.dot_general(
            own_rows, partner, (((1,), (1,)), ((), ())), preferred_element_type=jnp.float32
        )
        distance = row_sq[:, None] + col_sq[None, :] - 2.0 * gram_tile
        lagged_list.append(lag_sum(distance, LAG))
    partial_dist = jnp.stack(lagged_list)
    column_width = block_rows // lax.axis_size("space")
    start_col = lax.axis_index("space") * column_width
    summed_dist = lax.psum(partial_dist, "space")
    lagged = lax.dynamic_slice_in_dim(summed_dist, start_col, column_width, 2)
    total_cells = cells_dev * lax.axis_size("space")
    kernel = jnp.exp(-lagged / (LAG * total_cells * spread))
    degree = lax.psum(jnp.sum(kernel, axis=(0, 2)), "space")
    degree_list = [degree]
    current_degree = degree
    for offset in range(1, BANDS):
        current_degree = shifted(current_degree, "col", 1)
        degree_list.append(current_degree)
    column_degrees = lax.dynamic_slice_in_dim(jnp.stack(degree_list), start_col, column_width, 1)
    factor = float(BANDS * block_rows)
    return factor * kernel / jnp.sqrt(degree[None, :, None] * column_degrees[:, None, :])

CHUNK = 64
PIECE = 80


def gather_kernel(own, before, extra, start, tail, sent, got_before, got_extra, got_start, got_tail):
    row, slot, here = lax.axis_index("row"), lax.axis_index("col"), lax.axis_index("space")
    groups = lax.axis_size("row")
    rows = own.shape[0]
    first = rows - LAG
    n_chunk, n_piece = rows // CHUNK, LAG // PIECE
    barrier = pltpu.get_barrier_semaphore()

    def greet(group, place):
        pl.semaphore_signal(
            barrier, inc=1, device_id=(group, place, here), device_id_type=pl.DeviceIdType.MESH
        )

    def chunk(ref, c):
        return ref.at[pl.ds(c * CHUNK, CHUNK)]

    def piece(ref, p, offset=0):
        return ref.at[pl.ds(offset + p * PIECE, PIECE)]

    def copy(src, dst, kind, i, got, group, place):
        return pltpu.make_async_remote_copy(
            src_ref=src,
            dst_ref=dst,
            send_sem=sent.at[kind, i],
            recv_sem=got.at[i],
            device_id=(group, place, here),
            device_id_type=pl.DeviceIdType.MESH,
        )

    def send_chunk(src, dst, c, kind, got, place):
        made = copy(chunk(src, c), chunk(dst, c), kind, c, got, row, place)
        made.start()
        return made

    def send_piece(src, dst, p, kind, got, group, place, offset=0):
        made = copy(piece(src, p, offset), piece(dst, p), kind, p, got, group, place)
        made.start()
        return made

    def wait_chunk(dst, c, got):
        copy(chunk(dst, c), chunk(dst, c), 0, c, got, row, slot).wait_recv()

    def wait_piece(dst, p, got):
        copy(piece(dst, p), piece(dst, p), 0, p, got, row, slot).wait_recv()

    def all_sent(made):
        for one in made:
            one.wait_send()

    @pl.when(slot == 0)
    def _():
        greet(row, 1)
        pl.semaphore_wait(barrier, 1)
        made = [send_chunk(own, before, c, 0, got_before, 1) for c in range(n_chunk)]
        for c in range(n_chunk):
            wait_chunk(extra, c, got_extra)
        for p in range(n_piece):
            wait_piece(tail, p, got_tail)

        @pl.when(row > 0)
        def _():
            for p in range(n_piece):
                wait_piece(start, p, got_start)

        all_sent(made)

    @pl.when(slot == 1)
    def _():
        greet(row, 0)
        greet(row, 2)
        greet(row, 3)
        pl.semaphore_wait(barrier, 3)
        made = [send_chunk(own, before, c, 0, got_before, 2) for c in range(n_chunk)]
        turns = [((c + 1) * 11, 0, c) for c in range(n_chunk)]
        turns += [((c + 1) * 20, 1, c) for c in range(n_chunk)]
        turns += [((p + 1) * 30, 2, p) for p in range(n_piece)]
        turns += [(110 + p * 20, 3, p) for p in range(n_piece)]
        for _, kind, i in sorted(turns):
            if kind == 0:
                wait_chunk(before, i, got_before)
                made.append(send_chunk(before, extra, i, 2, got_extra, 2))
            elif kind == 1:
                wait_chunk(extra, i, got_extra)
                made.append(send_chunk(extra, extra, i, 1, got_extra, 0))
            elif kind == 2:
                wait_piece(tail, i, got_tail)
                made.append(send_piece(tail, tail, i, 3, got_tail, row, 0))
            else:

                @pl.when(row > 0)
                def _():
                    wait_piece(start, i, got_start)
                    send_piece(start, start, i, 4, got_start, row, 0)

        @pl.when(row > 0)
        def _():
            for p in range(n_piece):
                copy(piece(start, p), piece(start, p), 4, p, got_start, row, 0).wait_send()

        all_sent(made)

    @pl.when(slot == 2)
    def _():
        greet(row, 1)
        greet(row, 3)

        @pl.when(row > 0)
        def _():
            greet(row - 1, 3)

        pl.semaphore_wait(barrier, 2 + (row > 0).astype(jnp.int32))
        made = [send_piece(own, tail, p, 3, got_tail, row, 1, first) for p in range(n_piece)]
        made += [send_chunk(own, before, c, 0, got_before, 3) for c in range(n_chunk)]

        @pl.when(row > 0)
        def _():
            for p in range(n_piece):
                wait_piece(start, p, got_start)
                send_piece(start, start, p, 4, got_start, row, 1)

        for c in range(n_chunk):
            wait_chunk(before, c, got_before)
        made += [send_piece(before, tail, p, 1, got_tail, row, 3, first) for p in range(n_piece)]
        for c in range(n_chunk):
            wait_chunk(extra, c, got_extra)

        @pl.when(row > 0)
        def _():
            for p in range(n_piece):
                copy(piece(start, p), piece(start, p), 4, p, got_start, row, 1).wait_send()

        all_sent(made)

    @pl.when(slot == 3)
    def _():
        greet(row, 1)
        greet(row, 2)

        @pl.when(row < groups - 1)
        def _():
            greet(row + 1, 2)

        pl.semaphore_wait(barrier, 2 + (row < groups - 1).astype(jnp.int32))
        made = [send_chunk(own, extra, c, 0, got_extra, 1) for c in range(2)]

        @pl.when(row < groups - 1)
        def _():
            for p in range(n_piece):
                send_piece(own, start, p, 4, got_start, row + 1, 2, first)

        made += [send_chunk(own, extra, c, 0, got_extra, 1) for c in range(2, n_chunk)]

        for c in range(n_chunk):
            wait_chunk(before, c, got_before)
        for p in range(n_piece):
            wait_piece(tail, p, got_tail)

        @pl.when(row < groups - 1)
        def _():
            for p in range(n_piece):
                last = piece(own, p, first)
                copy(last, piece(start, p), 4, p, got_start, row + 1, 2).wait_send()

        all_sent(made)


def gather_blocks(masked):
    rows, cells = masked.shape
    n_chunk, n_piece = rows // CHUNK, LAG // PIECE
    block = jax.ShapeDtypeStruct((rows, cells), masked.dtype)
    part = jax.ShapeDtypeStruct((LAG, cells), masked.dtype)
    anywhere = pl.BlockSpec(memory_space=pl.ANY)
    return pl.pallas_call(
        gather_kernel,
        out_shape=[block, block, part, part],
        in_specs=[anywhere],
        out_specs=[anywhere] * 4,
        scratch_shapes=[
            pltpu.SemaphoreType.DMA((5, n_chunk)),
            pltpu.SemaphoreType.DMA((n_chunk,)),
            pltpu.SemaphoreType.DMA((n_chunk,)),
            pltpu.SemaphoreType.DMA((n_piece,)),
            pltpu.SemaphoreType.DMA((n_piece,)),
        ],
        compiler_params=pltpu.CompilerParams(collective_id=0, has_side_effects=True),
    )(masked)


def routed(block, axis, pairs):
    return lax.ppermute(block, axis, pairs)


def pick(condition, yes, no):
    return lax.select(jnp.broadcast_to(condition, yes.shape), yes, no)


def partial_lagged(rows, row_sq, columns, col_sq):
    gram = lax.dot_general(rows, columns, (((1,), (1,)), ((), ())), preferred_element_type=jnp.float32)
    distance = row_sq[:, None] + col_sq[None, :] - 2.0 * gram
    return lag_sum(distance, LAG)[1:, 1:]


def group_of_four(snapshots, ocean_mask, spread):
    block_rows, cells_dev = snapshots.shape
    spaces = lax.axis_size("space")
    width = block_rows // spaces
    slot = lax.axis_index("col")
    here = lax.axis_index("space")
    masked = snapshots * ocean_mask.astype(jnp.bfloat16)[None, :]
    before, extra, start, tail = gather_blocks(masked)
    start = pick(lax.axis_index("row") == 0, jnp.zeros_like(start), start)
    before_tail, extra_tail = before[block_rows - LAG :], extra[block_rows - LAG :]
    rows = jnp.concatenate([pick(slot == 0, start, before_tail), masked])
    next_tail = pick(slot == 1, start, pick(slot == 2, extra_tail, tail))
    next_rows = jnp.concatenate([next_tail, pick(slot == 0, extra, before)])
    last_rows = jnp.concatenate([pick(slot == 1, tail, start), extra])

    over = [(i, 1 - i) for i in range(2)]

    def halves(tile, dim):
        mine = lax.dynamic_slice_in_dim(tile, here * width, width, dim)
        other = lax.dynamic_slice_in_dim(tile, (1 - here) * width, width, dim)
        return mine + routed(other, "space", over)

    row_sq = square_norms(rows)
    lagged_0 = halves(partial_lagged(rows, row_sq, rows, row_sq), 1)
    lagged_1 = halves(partial_lagged(rows, row_sq, next_rows, square_norms(next_rows)), 1)
    tile_2 = partial_lagged(rows, row_sq, last_rows, square_norms(last_rows))
    turned = routed(halves(tile_2, 0), "col", [(1, 3), (2, 0)]).T
    inner = (slot == 1) | (slot == 2)
    lagged_2 = pick(inner, halves(tile_2, 1), turned)
    lagged = jnp.stack([lagged_0, lagged_1, lagged_2])

    kernel = jnp.exp(-lagged / (LAG * cells_dev * spaces * spread))
    half_degree = jnp.sum(kernel, axis=(0, 2))
    degree = half_degree + routed(half_degree, "space", over)
    degrees = [degree] + [shifted(degree, "col", offset) for offset in range(1, BANDS)]
    column_degrees = lax.dynamic_slice_in_dim(jnp.stack(degrees), here * width, width, 1)
    factor = float(BANDS * block_rows)
    return factor * kernel / jnp.sqrt(degree[None, :, None] * column_degrees[:, None, :])


def solution(mesh):
    placed = (P(("row", "col"), "space"), P("space"), P())
    four = mesh.shape["col"] == 4 and mesh.shape["space"] == 2
    return jax.shard_map(
        group_of_four if four else per_device,
        mesh=mesh,
        in_specs=placed,
        out_specs=P(None, ("row", "col"), "space"),
        check_vma=False,
    )
```
